32 devices in a mesh: seq: 4 (over y, x), bat: 8 (over z, core).
Axes of the slice: x: 2, y: 2, z: 4, core: 2. Of those that a mesh axis runs over, the one named last changes fastest.
Arguments:
- block_input: float32 [8, 2048, 1024], P('bat', 'seq'), may hold values from -6 to 6
- cotangent: float32 [8, 2048, 1024], P('bat', 'seq'), may hold values from -6 to 6
- lengths: int32 [8], P('bat'), may hold values from 1537 to 2048, as said below
- norm_gains: float32 [2, 1024], replicated, may hold values from 0.5 to 1.5
- chan_params: float32 [8, 1536], replicated, may hold values from -3 to 12, as said below
- gate_blocks: float32 [2, 8, 192, 192], replicated, may hold values from -0.4375 to 0.4375
- gains_first: float32 [2, 1024], replicated, may hold values from -24 to 24
- gains_second: float32 [2, 1024], replicated, may hold values from 39.3216 to 622.592
- chan_first: float32 [8, 1536], replicated, may hold values from -448 to 448
- chan_second: float32 [8, 1536], replicated, may hold values from 4096 to 131072
- gate_first: float32 [2, 8, 192, 192], replicated, may hold values from -24 to 24
- gate_second: float32 [2, 8, 192, 192], replicated, may hold values from 39.3216 to 622.592
- tile_weights: float32 [3456, 32, 128], P(('seq', 'bat')), may hold values from -0.1875 to 0.1875
- tile_first: float32 [3456, 32, 128], P(('seq', 'bat')), may hold values from -24 to 24
- tile_second: float32 [3456, 32, 128], P(('seq', 'bat')), may hold values from 39.3216 to 622.592
- basis_left: float32 [3456, 32, 32], P(('seq', 'bat')), may hold values from -1 to 1, as said below
- basis_right: float32 [3456, 128, 128], P(('seq', 'bat')), may hold values from -1 to 1, as said below
- stat_left: float32 [3456, 32, 32], P(('seq', 'bat')), may hold values from -2097152 to 2097152, as said below
- stat_right: float32 [3456, 128, 128], P(('seq', 'bat')), may hold values from -2097152 to 2097152, as said below
- tile_of_slot: int32 [3456], replicated, may hold values from 0 to 3455, each once
Outputs:
- block_output: float32 [8, 2048, 1024], P('bat', 'seq')
- input_grad: float32 [8, 2048, 1024], P('bat', 'seq')
- gains_first_new: float32 [2, 1024], replicated
- gains_second_new: float32 [2, 1024], replicated
- gains_new: float32 [2, 1024], replicated
- chan_first_new: float32 [8, 1536], replicated
- chan_second_new: float32 [8, 1536], replicated
- chan_new: float32 [8, 1536], replicated
- gate_first_new: float32 [2, 8, 192, 192], replicated
- gate_second_new: float32 [2, 8, 192, 192], replicated
- gate_new: float32 [2, 8, 192, 192], replicated
- tile_first_new: float32 [3456, 32, 128], P(('seq', 'bat'))
- tile_second_new: float32 [3456, 32, 128], P(('seq', 'bat'))
- tile_weights_new: float32 [3456, 32, 128], P(('seq', 'bat'))
- basis_left_new: float32 [3456, 32, 32], P(('seq', 'bat'))
- basis_right_new: float32 [3456, 128, 128], P(('seq', 'bat'))
- stat_left_new: float32 [3456, 32, 32], P(('seq', 'bat'))
- stat_right_new: float32 [3456, 128, 128], P(('seq', 'bat'))
The draws below stay inside these ranges and needn't reach their ends.
Inputs may be any that keep to these rules, and one draw needn't show every extreme that they name: `lengths`: every sequence has at least 1537 tokens; some sequence has exactly 2048. `tile_of_slot`: a permutation of the tile numbers. `chan_params`: the decay parameters of row 7 lie between 3.5 and 12. `basis_left`: each matrix is orthogonal. `basis_right`: each matrix is orthogonal. `stat_left`: each matrix is symmetric positive definite. `stat_right`: each matrix is symmetric positive definite.
All inputs are finite; a program needn't handle non-finite values.
Results may differ from the reference program's by a relative error of at most 0.008.
The reference program's roundings to bfloat16 on the way count: a program that leaves them out, or rounds other values in their place, can miss the bound.
Values may be sent and summed in bfloat16 or wider, within the bound.
A program may use at most 448 MiB of HBM per device.

```python
import math
import jax
import jax.numpy as jnp
from jax import lax

D = 1024
R = 1536
F = 3072
HB = 8
CONV = 4
TI = 32
TO = 128
STEPNUM = 10
TOK_DEV = 512
BS = 192
LEN = 2048
BATCH = 8
TOKENS = 16384
TILES = 3456


def draw_lengths(key, part):
    key = jax.random.fold_in(key, 11)
    first_key, second_key = jax.random.split(key)
    drawn = jax.random.randint(first_key, (BATCH,), LEN - TOK_DEV + 1, LEN + 1)
    chosen = jax.random.randint(second_key, (), 0, BATCH)
    return drawn.at[chosen].set(LEN).astype(jnp.int32)


def draw_chan_params(key, part):
    key = jax.random.fold_in(key, 12)
    tap_key, bias_key, gate_key, lambda_key = jax.random.split(key, 4)
    taps = 0.5 * jax.random.truncated_normal(tap_key, -3.0, 3.0, (CONV, R), jnp.float32)
    conv_bias = 0.5 * jax.random.truncated_normal(bias_key, -3.0, 3.0, (1, R), jnp.float32)
    gate_bias = jax.random.truncated_normal(gate_key, -3.0, 3.0, (2, R), jnp.float32)
    lambda_row = jax.random.uniform(lambda_key, (1, R), jnp.float32, 3.5, math.log(LEN) + 2.0)
    return jnp.concatenate([taps, conv_bias, gate_bias, lambda_row], axis=0)


def draw_chan_second(key, part):
    key = jax.random.fold_in(key, 17)
    factor = jnp.exp(jax.random.uniform(key, (CONV + 4, R), jnp.float32, math.log(0.5), math.log(8.0)))
    return factor * TOKENS


def orthogonal(key, dimension):
    sign_key, order_key, vector_key = jax.random.split(key, 3)
    rows = jnp.arange(dimension, dtype=jnp.float32)[:, None]
    cols = jnp.arange(dimension, dtype=jnp.float32)[None, :]
    table = jnp.cos(math.pi * (2.0 * cols + 1.0) * rows / (2.0 * dimension)) * math.sqrt(2.0 / dimension)
    table = jnp.where(rows == 0.0, table * math.sqrt(0.5), table)
    order_keys = jax.random.split(order_key, TILES)
    orders = jax.vmap(lambda single: jax.random.permutation(single, dimension))(order_keys)
    base = jnp.take(table, orders, axis=1)
    base = jnp.transpose(base, (1, 0, 2))
    vectors = jax.random.normal(vector_key, (TILES, dimension), jnp.float32)
    along = jnp.sum(vectors[:, :, None] * base, axis=1)
    lengths_sq = jnp.sum(vectors * vectors, axis=1)
    reflected = base - (2.0 / lengths_sq)[:, None, None] * vectors[:, :, None] * along[:, None, :]
    signs = 2.0 * jax.random.randint(sign_key, (TILES, dimension), 0, 2).astype(jnp.float32) - 1.0
    return reflected * signs[:, None, :]


def statistic(key, dimension, scale):
    diag_key, spread_key = jax.random.split(key)
    diagonal = scale * jnp.exp(jax.random.uniform(diag_key, (TILES, dimension), jnp.float32, 0.0, math.log(4.0)))
    spread = jax.random.uniform(spread_key, (TILES, dimension, dimension), jnp.float32, -1.0, 1.0)
    spread = 0.125 * scale / dimension * (spread + jnp.swapaxes(spread, 1, 2))
    identity = jnp.eye(dimension, dtype=jnp.float32)
    return spread * (1.0 - identity) + diagonal[:, :, None] * identity


def draw_basis_left(key, part):
    key = jax.random.fold_in(key, 13)
    return orthogonal(key, TI)


def draw_basis_right(key, part):
    key = jax.random.fold_in(key, 14)
    return orthogonal(key, TO)


def draw_stat_left(key, part):
    key = jax.random.fold_in(key, 15)
    return statistic(key, TI, 0.09 * TO * TOKENS)


def draw_stat_right(key, part):
    key = jax.random.fold_in(key, 16)
    return statistic(key, TO, 0.09 * TI * TOKENS)


def levels(own_key, dims, shards, least, top_value):
    def one(dim, blocks):
        steps = jax.random.uniform(jax.random.fold_in(jax.random.fold_in(own_key, 6), dim), (blocks,), jnp.float32, least / len(shards), top_value / len(shards))
        return jnp.repeat(jnp.exp(steps), dims[dim] // blocks).reshape((-1,) + (1,) * (len(dims) - dim - 1))

    gain = one(*shards[0])
    for cut in shards[1:]:
        gain = gain * one(*cut)
    return gain


def normal_values(rng, dims, scale, most, cuts=(), held_as=jnp.bfloat16):
    factor_of = levels(rng, dims, cuts, -0.22, 0.18) if cuts else 1.0
    result = jax.random.normal(rng, dims, jnp.float32) * scale * factor_of
    return jnp.minimum(jnp.maximum(result, -most), most).astype(held_as)


def setup_inputs(seed: int = 0) -> dict:
    keys = jax.random.split(jax.random.key(seed), 21)
    return {
        "block_input": normal_values(keys[0], (BATCH, LEN, D), 1.0, 6.0, ((0, 8), (1, 4)), jnp.float32),
        "cotangent": normal_values(keys[1], (BATCH, LEN, D), 1.0, 6.0, ((0, 8), (1, 4)), jnp.float32),
        "lengths": draw_lengths(jax.random.fold_in(keys[20], 71), 0),
        "norm_gains": jnp.clip(1.0 + 0.1 * jax.random.normal(keys[3], (2, D), jnp.float32), 0.5, 1.5),
        "chan_params": draw_chan_params(jax.random.fold_in(keys[20], 71), 0),
        "gate_blocks": normal_values(keys[5], (2, HB, BS, BS), BS ** -0.5, 0.4375, (), jnp.float32),
        "gains_first": normal_values(keys[6], (2, D), (0.033 * TOKENS ** 0.5), 24.0, (), jnp.float32),
        "gains_second": jnp.clip(jnp.exp(jax.random.uniform(keys[7], (2, D), jnp.float32, math.log(39.3216), math.log(622.592))), 39.3216, 622.592),
        "chan_first": normal_values(keys[8], (CONV + 4, R), (0.6 * TOKENS ** 0.5), 448.0, (), jnp.float32),
        "chan_second": draw_chan_second(jax.random.fold_in(keys[20], 71), 0),
        "gate_first": normal_values(keys[10], (2, HB, BS, BS), (0.033 * TOKENS ** 0.5), 24.0, (), jnp.float32),
        "gate_second": jnp.clip(jnp.exp(jax.random.uniform(keys[11], (2, HB, BS, BS), jnp.float32, math.log(39.3216), math.log(622.592))), 39.3216, 622.592),
        "tile_weights": normal_values(keys[12], (TILES, TI, TO), D ** -0.5, 0.1875, ((0, 32),), jnp.float32),
        "tile_first": normal_values(keys[13], (TILES, TI, TO), (0.033 * TOKENS ** 0.5), 24.0, ((0, 32),), jnp.float32),
        "tile_second": jnp.clip(jnp.exp(math.log(622.592) - 2.7621173 * jax.random.uniform(keys[14], (TILES, TI, TO), jnp.float32) ** levels(keys[14], (TILES, TI, TO), ((0, 32),), -0.2, 0.2)), 39.3216, 622.592),
        "basis_left": draw_basis_left(jax.random.fold_in(keys[20], 71), 0),
        "basis_right": draw_basis_right(jax.random.fold_in(keys[20], 71), 0),
        "stat_left": draw_stat_left(jax.random.fold_in(keys[20], 71), 0),
        "stat_right": draw_stat_right(jax.random.fold_in(keys[20], 71), 0),
        "tile_of_slot": jax.random.permutation(keys[19], TILES).astype(jnp.int32),
    }


@jax.custom_vjp
def low(v):
    return lax.optimization_barrier(v.astype(jnp.bfloat16)).astype(jnp.float32)

@jax.custom_vjp
def low_back(v):
    return v

def low_keep(v):
    return (low(v), None)

def low_pass(kept, grad):
    return (grad,)

def back_keep(v):
    return (v, None)

def back_low(kept, grad):
    return (low(grad),)
low.defvjp(low_keep, low_pass)
low_back.defvjp(back_keep, back_low)
highest = lax.Precision.HIGHEST
norm_eps = 1e-06
beta_one = 0.9
beta_two = 0.95
adam_eps = 1e-08
learn_rate = 0.02
small_rate = 0.5
decay_rate = 0.01
decay_scale = 8.0

def project(left_side, right_side):
    return jnp.dot(left_side.astype(jnp.float32), right_side.astype(jnp.float32), precision=highest, preferred_element_type=jnp.float32)

def rms_norm(values, gain_row):
    return values * lax.rsqrt(lax.optimization_barrier(jnp.mean(values * values, axis=-1, keepdims=True)) + norm_eps) * gain_row

def block_mix(values, blocks):
    split_view = values.reshape(values.shape[0], HB, BS)
    return jnp.einsum('tbi,bij->tbj', split_view, blocks, precision=highest).reshape(values.shape[0], R)

def causal_conv(values, chan_rows):
    length_here = values.shape[0]
    padded = jnp.concatenate([jnp.zeros((CONV - 1, R), jnp.float32), values], axis=0)
    summed = chan_rows[CONV] + jnp.zeros_like(values)
    for tap_index in range(CONV):
        summed = summed + chan_rows[tap_index] * padded[CONV - 1 - tap_index:CONV - 1 - tap_index + length_here]
    return summed

def gate_piece(mix_keep, mix_admit, conv_out, bias_keep, bias_admit, lambda_row):
    keep_gate = jax.nn.sigmoid(mix_keep + bias_keep)
    admit_gate = jax.nn.sigmoid(mix_admit + bias_admit)
    log_decay = -decay_scale * keep_gate * jax.nn.softplus(-lambda_row)
    decays = jnp.exp(log_decay)
    injects = jnp.sqrt(-jnp.expm1(2.0 * log_decay)) * admit_gate * conv_out
    return (decays, injects)

def combine_pairs(earlier, later):
    return (earlier[0] * later[0], later[0] * earlier[1] + later[1])

def forward_one(tokens, weights, gain_pair, chan_rows, gate_pair):
    input_weight, branch_weight, output_weight, gate_weight, upward_weight, down_weight = weights
    hidden_one = low(rms_norm(tokens, gain_pair[0]))
    conv_in = low_back(project(hidden_one, input_weight))
    branch_pre = low_back(project(hidden_one, branch_weight))
    branch = jax.nn.gelu(branch_pre)
    conv_out = low(causal_conv(conv_in, chan_rows))
    mix_keep = low_back(block_mix(conv_out, gate_pair[0]))
    mix_admit = low_back(block_mix(conv_out, gate_pair[1]))
    decays, injects = gate_piece(mix_keep, mix_admit, conv_out, chan_rows[CONV + 1], chan_rows[CONV + 2], chan_rows[CONV + 3])
    states = lax.associative_scan(combine_pairs, (decays, injects), axis=0)[1]
    mixed_low = low(states * branch)
    residual_mid = tokens + low_back(project(mixed_low, output_weight))
    hidden_two = low(rms_norm(residual_mid, gain_pair[1]))
    gate_pre = low_back(project(hidden_two, gate_weight))
    upward_pre = low_back(project(hidden_two, upward_weight))
    mlp_low = low(jax.nn.gelu(gate_pre) * upward_pre)
    return residual_mid + low_back(project(mlp_low, down_weight))

def whole(block_input, weights, gain_pair, chan_rows, gate_pair):
    lowered = tuple((low(matrix) for matrix in weights))
    gates_low = low(gate_pair)
    checked = jax.checkpoint(forward_one)
    return lax.map(lambda tokens: checked(tokens, lowered, gain_pair, chan_rows, gates_low), block_input)

def matrix_shapes():
    return ((D, R), (D, R), (R, D), (D, F), (D, F), (F, D))

def tiles_to_matrices(tiles):
    matrices = []
    offset = 0
    for row_count, col_count in matrix_shapes():
        tile_count = row_count // TI * (col_count // TO)
        tile_block = tiles[offset:offset + tile_count].reshape(row_count // TI, col_count // TO, TI, TO)
        matrices.append(tile_block.transpose(0, 2, 1, 3).reshape(row_count, col_count))
        offset = offset + tile_count
    return tuple(matrices)

def matrices_to_tiles(matrices):
    pieces = []
    for matrix in matrices:
        row_count, col_count = matrix.shape
        pieces.append(matrix.reshape(row_count // TI, TI, col_count // TO, TO).transpose(0, 2, 1, 3).reshape(-1, TI, TO))
    return jnp.concatenate(pieces, axis=0)

def cholesky_qr(product):
    gram = jnp.einsum('nij,nik->njk', product, product, precision=highest)
    factor = jnp.linalg.cholesky(gram)
    return lax.linalg.triangular_solve(factor, product, left_side=False, lower=True, transpose_a=True)

def soap_update(grads, first, second, weight, basis_l, basis_r, stat_l, stat_r):
    rotated = jnp.einsum('nij,nik,nkl->njl', basis_l, grads, basis_r, precision=highest)
    first_new = beta_one * first + (1.0 - beta_one) * rotated
    second_new = beta_two * second + (1.0 - beta_two) * rotated * rotated
    direction = first_new / (1.0 - beta_one ** STEPNUM) / (jnp.sqrt(second_new / (1.0 - beta_two ** STEPNUM)) + adam_eps)
    update = jnp.einsum('nij,njk,nlk->nil', basis_l, direction, basis_r, precision=highest)
    weight_new = weight - learn_rate * (update + decay_rate * weight)
    stat_l_new = beta_two * stat_l + (1.0 - beta_two) * jnp.einsum('nij,nkj->nik', grads, grads, precision=highest)
    stat_r_new = beta_two * stat_r + (1.0 - beta_two) * jnp.einsum('nji,njk->nik', grads, grads, precision=highest)
    basis_l_new = cholesky_qr(jnp.einsum('nij,njk->nik', stat_l_new, basis_l, precision=highest))
    basis_r_new = cholesky_qr(jnp.einsum('nij,njk->nik', stat_r_new, basis_r, precision=highest))
    return (first_new, second_new, weight_new, basis_l_new, basis_r_new, stat_l_new, stat_r_new)

def adam_update(grads, first, second, weight, rate):
    first_new = beta_one * first + (1.0 - beta_one) * grads
    second_new = beta_two * second + (1.0 - beta_two) * grads * grads
    direction = first_new / (1.0 - beta_one ** STEPNUM) / (jnp.sqrt(second_new / (1.0 - beta_two ** STEPNUM)) + adam_eps)
    return (first_new, second_new, weight - rate * direction)

def reference(block_input, cotangent, lengths, norm_gains, chan_params, gate_blocks, gains_first, gains_second, chan_first, chan_second, gate_first, gate_second, tile_weights, tile_first, tile_second, basis_left, basis_right, stat_left, stat_right, tile_of_slot):
    slot_numbers = jnp.arange(TILES, dtype=jnp.int32)
    inverse = jnp.zeros((TILES,), jnp.int32).at[tile_of_slot].set(slot_numbers)
    matrices = tiles_to_matrices(tile_weights[inverse])
    block_output, pullback = jax.vjp(whole, block_input, matrices, norm_gains, chan_params, gate_blocks)
    positions = jnp.arange(LEN, dtype=jnp.int32)
    valid_mask = (positions[None, :] < lengths[:, None]).astype(jnp.float32)
    input_grad, matrix_grads, gains_grad, chan_grad, gates_grad = pullback(cotangent * valid_mask[:, :, None])
    tile_grads = matrices_to_tiles(matrix_grads)[tile_of_slot]
    soap_out = soap_update(tile_grads, tile_first, tile_second, tile_weights, basis_left, basis_right, stat_left, stat_right)
    gains_out = adam_update(gains_grad, gains_first, gains_second, norm_gains, small_rate)
    chan_out = adam_update(chan_grad, chan_first, chan_second, chan_params, small_rate)
    gate_out = adam_update(gates_grad, gate_first, gate_second, gate_blocks, learn_rate)
    return (block_output, input_grad, gains_out[0], gains_out[1], gains_out[2], chan_out[0], chan_out[1], chan_out[2], gate_out[0], gate_out[1], gate_out[2], soap_out[0], soap_out[1], soap_out[2], soap_out[3], soap_out[4], soap_out[5], soap_out[6])
```

```python
import functools

import jax
import jax.numpy as jnp
from jax import lax
from jax.experimental import pallas as pl
from jax.experimental.pallas import tpu as pltpu
from jax.sharding import PartitionSpec as P

D = 1024
R = 1536
F = 3072
HB = 8
CONV = 4
TI = 32
TO = 128
STEPNUM = 10
BS = 192
GC = 384
LANES = GC // 128
SEG = 8
f32 = jnp.float32
bf16 = jnp.bfloat16


highest = lax.Precision.HIGHEST
norm_eps = 1e-06
beta_one = 0.9
beta_two = 0.95
adam_eps = 1e-08
learn_rate = 0.02
small_rate = 0.5
decay_rate = 0.01
decay_scale = 8.0


def entering(factor, total, axis, reverse):
    count = lax.axis_size(axis)
    place = lax.axis_index(axis)
    gathered = lax.all_gather(jnp.stack([factor, total]), axis)
    state = jnp.zeros_like(total)
    for step in range(count):
        source = count - 1 - step if reverse else step
        passed = source > place if reverse else source < place
        state = jnp.where(passed, gathered[source, 1] + gathered[source, 0] * state, state)
    return state


def passed_along(value, axis, by):
    devices = lax.axis_size(axis)
    pairs = [(i, i + by) for i in range(devices) if 0 <= i + by < devices]
    return lax.ppermute(value, axis, pairs)


def multiply(left_side, matrix):
    return jnp.dot(left_side, matrix, preferred_element_type=jnp.float32)


def multiply_transposed(left_side, matrix):
    return jnp.einsum("tj,ij->ti", left_side, matrix, preferred_element_type=jnp.float32)


def contract_rows(left_side, right_side):
    return jnp.einsum("ti,tj->ij", left_side, right_side, preferred_element_type=jnp.float32)


def rms_norm(values, gain_row):
    return (
        values * lax.rsqrt(jnp.mean(values * values, axis=-1, keepdims=True) + norm_eps) * gain_row
    )


def gate_values(conv_low, keep_block, admit_block, rows):
    mix_keep = jnp.dot(conv_low, keep_block, preferred_element_type=f32)
    mix_admit = jnp.dot(conv_low, admit_block, preferred_element_type=f32)
    keep_gate = jax.nn.sigmoid(mix_keep + rows[CONV + 1 : CONV + 2])
    admit_gate = jax.nn.sigmoid(mix_admit + rows[CONV + 2 : CONV + 3])
    log_decay = (-decay_scale * rows[CONV + 3 : CONV + 4]) * keep_gate
    decays = jnp.exp(log_decay)
    twice = 2.0 * log_decay
    series = 1.0 + twice * (1.0 / 7.0)
    for order in (6.0, 5.0, 4.0, 3.0, 2.0):
        series = 1.0 + twice * (1.0 / order) * series
    drop = jnp.where(twice > -0.4, -twice * series, 1.0 - decays * decays)
    return keep_gate, admit_gate, decays, drop

def forward_kernel(conv_in_ref, edge_ref, rows_ref, keep_ref, admit_ref,
                   conv_low_ref, decays_ref, prod_ref, local_ref, padded, factors, terms):
    tokens = conv_in_ref.shape[0]
    rows = rows_ref[...]
    padded[0:8, :] = edge_ref[...]
    padded[pl.ds(8, tokens), :] = conv_in_ref[...]
    conv = rows[CONV : CONV + 1] + rows[0:1] * conv_in_ref[...]
    for tap in range(1, CONV):
        conv += rows[tap : tap + 1] * padded[pl.ds(8 - tap, tokens), :]
    conv_low = conv.astype(bf16)
    conv_low_ref[...] = conv_low
    keep_gate, admit_gate, decays, drop = gate_values(conv_low, keep_ref[0], admit_ref[0], rows)
    decays_ref[...] = decays
    injects = jnp.sqrt(drop) * admit_gate * conv_low.astype(f32)
    for part in range(LANES):
        factors[pl.ds(part * tokens, tokens), :] = decays[:, part * 128 : part * 128 + 128]
        terms[pl.ds(part * tokens, tokens), :] = injects[:, part * 128 : part * 128 + 128]
    length = tokens // SEG

    def one(t, carry):
        result = []
        for part in range(LANES):
            prod, local = carry[part]
            at = pl.ds(part * tokens + t, SEG, stride=length)
            decay = factors[at, :]
            prod = prod * decay
            local = decay * local + terms[at, :]
            factors[at, :] = prod
            terms[at, :] = local
            result.append((prod, local))
        return tuple(result)

    start = (jnp.ones((SEG, 128), f32), jnp.zeros((SEG, 128), f32))
    lax.fori_loop(0, length, one, (start,) * LANES, unroll=8)
    for part in range(LANES):
        prod_ref[:, part * 128 : part * 128 + 128] = factors[pl.ds(part * tokens, tokens), :]
        local_ref[:, part * 128 : part * 128 + 128] = terms[pl.ds(part * tokens, tokens), :]

def col(block_rows):
    return pl.BlockSpec((block_rows, GC), lambda g: (0, g))

def mat():
    return pl.BlockSpec((1, GC, GC), lambda g: (g, 0, 0))

def recurrent_forward(conv_in, edge, rows, keep_blocks, admit_blocks):
    tokens = conv_in.shape[0]
    full = lambda dt: jax.ShapeDtypeStruct((tokens, R), dt)
    return pl.pallas_call(
        forward_kernel,
        grid=(R // GC,),
        out_shape=(full(bf16), full(f32), full(f32), full(f32)),
        in_specs=[col(tokens), col(8), col(8), mat(), mat()],
        out_specs=[col(tokens)] * 4,
        scratch_shapes=[pltpu.VMEM((tokens + 8, GC), f32)] + [pltpu.VMEM((LANES * tokens, 128), f32)] * 2,
        compiler_params=pltpu.CompilerParams(vmem_limit_bytes=48 * 2**20),
        name="recurrence_forward",
    )(conv_in, edge, rows, keep_blocks, admit_blocks)

def reverse_kernel(decays_ref, source_ref, prod_ref, local_ref, padded, factors, terms):
    tokens = decays_ref.shape[0]
    length = tokens // SEG
    padded[pl.ds(0, tokens), :] = decays_ref[...]
    padded[pl.ds(tokens, 8), :] = jnp.ones((8, decays_ref.shape[1]), f32)
    for part in range(LANES):
        factors[pl.ds(part * tokens, tokens), :] = padded[pl.ds(1, tokens), part * 128 : part * 128 + 128]
        terms[pl.ds(part * tokens, tokens), :] = source_ref[:, part * 128 : part * 128 + 128]

    def one(step, carry):
        result = []
        for part in range(LANES):
            prod, local = carry[part]
            at = pl.ds(part * tokens + length - 1 - step, SEG, stride=length)
            decay = factors[at, :]
            prod = prod * decay
            local = decay * local + terms[at, :]
            factors[at, :] = prod
            terms[at, :] = local
            result.append((prod, local))
        return tuple(result)

    start = (jnp.ones((SEG, 128), f32), jnp.zeros((SEG, 128), f32))
    lax.fori_loop(0, length, one, (start,) * LANES, unroll=8)
    for part in range(LANES):
        prod_ref[:, part * 128 : part * 128 + 128] = factors[pl.ds(part * tokens, tokens), :]
        local_ref[:, part * 128 : part * 128 + 128] = terms[pl.ds(part * tokens, tokens), :]

def recurrent_reverse(decays, source):
    tokens = decays.shape[0]
    full = jax.ShapeDtypeStruct((tokens, R), f32)
    return pl.pallas_call(
        reverse_kernel,
        grid=(R // GC,),
        out_shape=(full, full),
        in_specs=[col(tokens)] * 2,
        out_specs=[col(tokens)] * 2,
        scratch_shapes=[pltpu.VMEM((tokens + 8, GC), f32)] + [pltpu.VMEM((LANES * tokens, 128), f32)] * 2,
        compiler_params=pltpu.CompilerParams(vmem_limit_bytes=48 * 2**20),
        name="recurrence_reverse",
    )(decays, source)

def spread(carry, tokens):
    length = tokens // SEG
    return jnp.concatenate(
        [jnp.broadcast_to(carry[s : s + 1], (length, carry.shape[1])) for s in range(SEG)], axis=0)

def gate_back_kernel(conv_low_ref, states_ref, before_ref, prod_ref, local_ref, carry_ref, rows_ref,
                     keep_ref, admit_ref, conv_grad_ref, keep_grad_ref, admit_grad_ref, sums_ref, padded):
    tokens = conv_low_ref.shape[0]
    rows = rows_ref[...]
    conv_low = conv_low_ref[...]
    conv_out = conv_low.astype(f32)
    keep_gate, admit_gate, decays, drop = gate_values(conv_low, keep_ref[0], admit_ref[0], rows)
    padded[0:8, :] = before_ref[...]
    padded[pl.ds(8, tokens), :] = states_ref[...]
    state_grad = local_ref[...] + prod_ref[...] * spread(carry_ref[...], tokens)
    decay_grad = state_grad * padded[pl.ds(7, tokens), :]
    root = jnp.sqrt(drop)
    scaled = state_grad * conv_out
    root_grad = scaled * admit_gate
    log_grad = decay_grad * decays - root_grad * (decays * decays) / root
    keep_grad = log_grad * (-decay_scale * rows[CONV + 3 : CONV + 4]) * (keep_gate * (1.0 - keep_gate))
    admit_grad = scaled * root * (admit_gate * (1.0 - admit_gate))
    sums_ref[0:1, :] = jnp.sum(keep_grad, axis=0, keepdims=True)
    sums_ref[1:2, :] = jnp.sum(admit_grad, axis=0, keepdims=True)
    sums_ref[2:3, :] = jnp.sum(log_grad * keep_gate, axis=0, keepdims=True) * -decay_scale
    sums_ref[3:8, :] = jnp.zeros((5, rows.shape[1]), f32)
    keep_low = keep_grad.astype(bf16)
    admit_low = admit_grad.astype(bf16)
    back = (((1,), (1,)), ((), ()))
    over = (((0,), (0,)), ((), ()))
    conv_grad_ref[...] = (
        state_grad * root * admit_gate
        + lax.dot_general(keep_low, keep_ref[0], back, preferred_element_type=f32)
        + lax.dot_general(admit_low, admit_ref[0], back, preferred_element_type=f32)
    )
    keep_grad_ref[0] = lax.dot_general(conv_low, keep_low, over, preferred_element_type=f32)
    admit_grad_ref[0] = lax.dot_general(conv_low, admit_low, over, preferred_element_type=f32)

def gates_backward(conv_low, states, before, prod, local, carry, rows, keep_blocks, admit_blocks):
    tokens = conv_low.shape[0]
    blocks = jax.ShapeDtypeStruct((R // GC, GC, GC), f32)
    return pl.pallas_call(
        gate_back_kernel,
        grid=(R // GC,),
        out_shape=(jax.ShapeDtypeStruct((tokens, R), f32), blocks, blocks, jax.ShapeDtypeStruct((8, R), f32)),
        in_specs=[col(tokens), col(tokens), col(8), col(tokens), col(tokens), col(8), col(8), mat(), mat()],
        out_specs=[col(tokens), mat(), mat(), col(8)],
        scratch_shapes=[pltpu.VMEM((tokens + 8, GC), f32)],
        compiler_params=pltpu.CompilerParams(vmem_limit_bytes=56 * 2**20),
        name="gates_backward",
    )(conv_low, states, before, prod, local, carry, rows, keep_blocks, admit_blocks)

def conv_back_kernel(conv_grad_ref, after_ref, conv_in_ref, before_ref, rows_ref, low_ref, sums_ref, ahead, behind):
    tokens = conv_grad_ref.shape[0]
    rows = rows_ref[...]
    grads = conv_grad_ref[...]
    ahead[pl.ds(0, tokens), :] = grads
    ahead[pl.ds(tokens, 8), :] = after_ref[...]
    behind[0:8, :] = before_ref[...]
    behind[pl.ds(8, tokens), :] = conv_in_ref[...]
    total = rows[0:1] * grads
    sums_ref[0:1, :] = jnp.sum(grads * conv_in_ref[...], axis=0, keepdims=True)
    for tap in range(1, CONV):
        total += rows[tap : tap + 1] * ahead[pl.ds(tap, tokens), :]
        sums_ref[tap : tap + 1, :] = jnp.sum(grads * behind[pl.ds(8 - tap, tokens), :], axis=0, keepdims=True)
    sums_ref[CONV : CONV + 1, :] = jnp.sum(grads, axis=0, keepdims=True)
    sums_ref[CONV + 1 : 8, :] = jnp.zeros((7 - CONV, rows.shape[1]), f32)
    low_ref[...] = total.astype(bf16)

def conv_backward(conv_grad, after, conv_in, before, rows):
    tokens = conv_grad.shape[0]
    return pl.pallas_call(
        conv_back_kernel,
        grid=(R // GC,),
        out_shape=(jax.ShapeDtypeStruct((tokens, R), bf16), jax.ShapeDtypeStruct((8, R), f32)),
        in_specs=[col(tokens), col(8), col(tokens), col(8), col(8)],
        out_specs=[col(tokens), col(8)],
        scratch_shapes=[pltpu.VMEM((tokens + 8, GC), f32)] * 2,
        compiler_params=pltpu.CompilerParams(vmem_limit_bytes=48 * 2**20),
        name="conv_backward",
    )(conv_grad, after, conv_in, before, rows)

def pair_blocks(blocks):
    per = GC // BS
    grouped = blocks.reshape(HB // per, per, BS, BS)
    zero = jnp.zeros((HB // per, BS, BS), blocks.dtype)
    lines = [jnp.concatenate([grouped[:, i] if i == j else zero for j in range(per)], axis=2) for i in range(per)]
    return jnp.concatenate(lines, axis=1)

def unpair_blocks(paired):
    per = GC // BS
    parts = [paired[:, i * BS : (i + 1) * BS, i * BS : (i + 1) * BS] for i in range(per)]
    return jnp.stack(parts, axis=1).reshape(HB, BS, BS)


def mlp_act(gate_in, upward_in):
    return jax.nn.gelu(gate_in) * upward_in


def matrix_shapes():
    return ((D, R), (D, R), (R, D), (D, F), (D, F), (F, D))


def split_tiles(tiles):
    matrices = []
    offset = 0
    for row_count, col_count in matrix_shapes():
        tile_count = row_count // TI * (col_count // TO)
        tile_block = tiles[offset : offset + tile_count].reshape(
            row_count // TI, col_count // TO, TI, TO
        )
        matrices.append(tile_block.transpose(0, 2, 1, 3).reshape(row_count, col_count))
        offset = offset + tile_count
    return tuple(matrices)


def join_tiles(matrices):
    pieces = []
    for matrix in matrices:
        row_count, col_count = matrix.shape
        pieces.append(
            matrix.reshape(row_count // TI, TI, col_count // TO, TO)
            .transpose(0, 2, 1, 3)
            .reshape(-1, TI, TO)
        )
    return jnp.concatenate(pieces, axis=0)


def chol_kernel(n, count, g_ref, m_ref, q_ref, aug, mult, winv):
    nb = n // 8
    lanes = 128
    padrows = lanes - count
    sub = lax.broadcasted_iota(jnp.int32, (n, lanes), 0)
    def load(i, c):
        x = g_ref[pl.ds(i, count, stride=n), :]
        if padrows:
            x = jnp.concatenate([x, jnp.zeros((padrows, n), f32)], axis=0)
        aug[i, 0:n, :] = x.T
        aug[i, n:2*n, :] = jnp.where(sub == i, 1.0, 0.0)
        return c
    lax.fori_loop(0, n, load, 0)

    def step(kb, c):
        k0 = pl.multiple_of(kb * 8, 8)
        for r in range(8):
            d = aug[k0 + r, pl.ds(k0 + r, 1), :]
            inv = jnp.broadcast_to(lax.rsqrt(d), (8, lanes))
            ms = [jnp.broadcast_to(aug[k0 + r, pl.ds(k0 + r2, 1), :], (8, lanes)) * inv for r2 in range(r + 1, 8)]
            def prow(j, c, r=r, inv=inv, ms=ms):
                j0 = pl.multiple_of((kb + j) * 8, 8)
                u = aug[k0 + r, pl.ds(j0, 8), :] * inv
                aug[k0 + r, pl.ds(j0, 8), :] = u
                for q, r2 in enumerate(range(r + 1, 8)):
                    aug[k0 + r2, pl.ds(j0, 8), :] -= ms[q] * u
                return c
            lax.fori_loop(0, nb + 1, prow, 0, unroll=True)
        def rows(ib, c):
            i0 = pl.multiple_of(ib * 8, 8)
            for r in range(8):
                for a in range(8):
                    mult[r * 8 + a] = jnp.broadcast_to(aug[k0 + r, pl.ds(i0 + a, 1), :], (8, lanes))
            def cols(j, c):
                j0 = pl.multiple_of(j * 8, 8)
                us = [aug[k0 + r, pl.ds(j0, 8), :] for r in range(8)]
                for a in range(8):
                    t = aug[i0 + a, pl.ds(j0, 8), :]
                    p0 = mult[a] * us[0]
                    p1 = mult[8 + a] * us[1]
                    for r in range(2, 8, 2):
                        p0 += mult[r * 8 + a] * us[r]
                        p1 += mult[r * 8 + 8 + a] * us[r + 1]
                    aug[i0 + a, pl.ds(j0, 8), :] = t - (p0 + p1)
                return c
            lax.fori_loop(ib, nb + kb + 1, cols, 0)
            return c
        lax.fori_loop(kb + 1, nb, rows, 0)
        return c
    lax.fori_loop(0, nb, step, 0)

    def store(i, c):
        w = aug[i, n:2*n, :].T
        winv[pl.ds(i, count, stride=n), :] = w[:count]
        return c
    lax.fori_loop(0, n, store, 0)

    def apply(b, c):
        rows = pl.ds(pl.multiple_of(b * n, n), n)
        q_ref[rows, :] = lax.dot_general(m_ref[rows, :], winv[rows, :], (((1,), (1,)), ((), ())),
            precision=lax.Precision.HIGHEST, preferred_element_type=f32)
        return c
    lax.fori_loop(0, count, apply, 0, unroll=4 if count % 4 == 0 else 1)

def chol_qr(gram, m):
    count, n, _ = gram.shape
    out = pl.pallas_call(
        functools.partial(chol_kernel, n, count),
        out_shape=jax.ShapeDtypeStruct((count * n, n), f32),
        in_specs=[pl.BlockSpec(memory_space=pltpu.VMEM)] * 2,
        out_specs=pl.BlockSpec(memory_space=pltpu.VMEM),
        scratch_shapes=[pltpu.VMEM((n, 2 * n, 128), f32), pltpu.VMEM((64, 8, 128), f32), pltpu.VMEM((count * n, n), f32)],
        compiler_params=pltpu.CompilerParams(vmem_limit_bytes=60 * 2**20),
    )(gram.reshape(count * n, n), m.reshape(count * n, n))
    return out.reshape(count, n, n)


def cholesky_qr(product):
    gram = jnp.einsum("nij,nik->njk", product, product, precision=highest)
    return chol_qr(gram, product)


def soap_update(grads, first, second, weight, basis_l, basis_r, stat_l, stat_r):
    rotated = jnp.einsum("nij,nik,nkl->njl", basis_l, grads, basis_r, precision=highest)
    first_new = beta_one * first + (1.0 - beta_one) * rotated
    second_new = beta_two * second + (1.0 - beta_two) * rotated * rotated
    direction = (
        first_new
        / (1.0 - beta_one**STEPNUM)
        / (jnp.sqrt(second_new / (1.0 - beta_two**STEPNUM)) + adam_eps)
    )
    update = jnp.einsum("nij,njk,nlk->nil", basis_l, direction, basis_r, precision=highest)
    weight_new = weight - learn_rate * (update + decay_rate * weight)
    stat_l_new = beta_two * stat_l + (1.0 - beta_two) * jnp.einsum(
        "nij,nkj->nik", grads, grads, precision=highest
    )
    stat_r_new = beta_two * stat_r + (1.0 - beta_two) * jnp.einsum(
        "nji,njk->nik", grads, grads, precision=highest
    )
    basis_l_new = cholesky_qr(jnp.einsum("nij,njk->nik", stat_l_new, basis_l, precision=highest))
    basis_r_new = cholesky_qr(jnp.einsum("nij,njk->nik", stat_r_new, basis_r, precision=highest))
    return (first_new, second_new, weight_new, basis_l_new, basis_r_new, stat_l_new, stat_r_new)


def adam_update(grads, first, second, weight, rate):
    first_new = beta_one * first + (1.0 - beta_one) * grads
    second_new = beta_two * second + (1.0 - beta_two) * grads * grads
    direction = (
        first_new
        / (1.0 - beta_one**STEPNUM)
        / (jnp.sqrt(second_new / (1.0 - beta_two**STEPNUM)) + adam_eps)
    )
    return (first_new, second_new, weight - rate * direction)


def on_device(
    block_input,
    cotangent,
    lengths,
    norm_gains,
    chan_params,
    gate_blocks,
    gains_first,
    gains_second,
    chan_first,
    chan_second,
    gate_first,
    gate_second,
    tile_weights,
    tile_first,
    tile_second,
    basis_left,
    basis_right,
    stat_left,
    stat_right,
    tile_of_slot,
):
    tokens = block_input[0]
    token_count = tokens.shape[0]
    place_index = lax.axis_index("seq")
    positions = place_index * token_count + jnp.arange(token_count, dtype=jnp.int32)
    valid_mask = (positions < lengths[0]).astype(jnp.float32)[:, None]
    gathered = lax.all_gather(tile_weights.astype(jnp.bfloat16), ("seq", "bat"), axis=0, tiled=True)
    tile_total = gathered.shape[0]
    inverse = (
        jnp.zeros((tile_total,), jnp.int32)
        .at[tile_of_slot]
        .set(jnp.arange(tile_total, dtype=jnp.int32))
    )
    input_weight, branch_weight, output_weight, gate_weight, upward_weight, down_weight = (
        split_tiles(jnp.take(gathered, inverse, axis=0, mode="clip"))
    )
    gates_low = gate_blocks.astype(jnp.bfloat16)
    first_gain = norm_gains[0]
    second_gain = norm_gains[1]
    hidden_one = rms_norm(tokens, first_gain).astype(jnp.bfloat16)
    conv_in = multiply(hidden_one, input_weight)
    branch_pre = multiply(hidden_one, branch_weight)
    branch, branch_back = jax.vjp(jax.nn.gelu, branch_pre)
    rows = jnp.concatenate([chan_params[: CONV + 3], jax.nn.softplus(-chan_params[CONV + 3 :])], axis=0)
    keep_blocks, admit_blocks = pair_blocks(gates_low[0]), pair_blocks(gates_low[1])
    edge_rows = passed_along(conv_in[token_count - (CONV - 1) :], "seq", 1)
    edge_rows = jnp.pad(edge_rows, ((9 - CONV, 0), (0, 0)))
    conv_low, decays, product, local_state = recurrent_forward(
        conv_in, edge_rows, rows, keep_blocks, admit_blocks
    )
    length = token_count // SEG
    factors = [product[(s + 1) * length - 1] for s in range(SEG)]
    totals = [local_state[(s + 1) * length - 1] for s in range(SEG)]
    factor, total = factors[0], totals[0]
    for s in range(1, SEG):
        factor, total = factor * factors[s], totals[s] + factors[s] * total
    state_in = entering(factor, total, "seq", False)
    carries = [state_in]
    for s in range(SEG - 1):
        carries.append(totals[s] + factors[s] * carries[-1])
    states = local_state + product * spread(jnp.stack(carries), token_count)
    mixed_low = (states * branch).astype(jnp.bfloat16)
    residual_mid = tokens + multiply(mixed_low, output_weight)
    hidden_two = rms_norm(residual_mid, second_gain).astype(jnp.bfloat16)
    gate_pre = multiply(hidden_two, gate_weight)
    upward_pre = multiply(hidden_two, upward_weight)
    mlp_value, mlp_back = jax.vjp(mlp_act, gate_pre, upward_pre)
    mlp_low = mlp_value.astype(jnp.bfloat16)
    block_output = residual_mid + multiply(mlp_low, down_weight)
    masked_grad = cotangent[0] * valid_mask
    masked_low = masked_grad.astype(jnp.bfloat16)
    down_weight_grad = contract_rows(mlp_low, masked_low)
    grad_mlp = multiply_transposed(masked_low, down_weight)
    grad_gate_pre, grad_upward_pre = mlp_back(grad_mlp)
    gate_grad_low = grad_gate_pre.astype(jnp.bfloat16)
    upward_grad_low = grad_upward_pre.astype(jnp.bfloat16)
    gate_weight_grad = contract_rows(hidden_two, gate_grad_low)
    upward_weight_grad = contract_rows(hidden_two, upward_grad_low)
    grad_hidden_two = multiply_transposed(gate_grad_low, gate_weight) + multiply_transposed(
        upward_grad_low, upward_weight
    )
    norm_two_out, norm_two_back = jax.vjp(rms_norm, residual_mid, second_gain)
    grad_mid_norm, second_gain_grad = norm_two_back(grad_hidden_two)
    grad_mid = masked_grad + grad_mid_norm
    mid_low = grad_mid.astype(jnp.bfloat16)
    output_weight_grad = contract_rows(mixed_low, mid_low)
    grad_mixed = multiply_transposed(mid_low, output_weight)
    branch_grad_low = branch_back(grad_mixed * states)[0].astype(jnp.bfloat16)
    back_product, local_grad = recurrent_reverse(decays, grad_mixed * branch)
    factors = [back_product[s * length] for s in range(SEG)]
    totals = [local_grad[s * length] for s in range(SEG)]
    factor, total = factors[-1], totals[-1]
    for s in range(SEG - 2, -1, -1):
        factor, total = factor * factors[s], totals[s] + factors[s] * total
    grad_in = entering(decays[0] * factor, decays[0] * total, "seq", True)
    carries = [grad_in]
    for s in range(SEG - 1, 0, -1):
        carries.append(totals[s] + factors[s] * carries[-1])
    before = jnp.pad(state_in[None], ((7, 0), (0, 0)))
    conv_grad, keep_paired, admit_paired, gate_sums = gates_backward(
        conv_low, states, before, back_product, local_grad, jnp.stack(carries[::-1]), rows,
        keep_blocks, admit_blocks,
    )
    gate_blocks_grad = jnp.stack([unpair_blocks(keep_paired), unpair_blocks(admit_paired)])
    edge_grads = passed_along(conv_grad[: CONV - 1], "seq", -1)
    edge_grads = jnp.pad(edge_grads, ((0, 9 - CONV), (0, 0)))
    conv_in_low, conv_sums = conv_backward(conv_grad, edge_grads, conv_in, edge_rows, rows)
    lambda_grad = -jax.nn.sigmoid(-chan_params[CONV + 3 :]) * gate_sums[2:3]
    input_weight_grad = contract_rows(hidden_one, conv_in_low)
    branch_weight_grad = contract_rows(hidden_one, branch_grad_low)
    grad_hidden_one = multiply_transposed(conv_in_low, input_weight) + multiply_transposed(
        branch_grad_low, branch_weight
    )
    norm_one_out, norm_one_back = jax.vjp(rms_norm, tokens, first_gain)
    grad_tokens_norm, first_gain_grad = norm_one_back(grad_hidden_one)
    input_grad = grad_mid + grad_tokens_norm
    small_terms = (
        jnp.stack([first_gain_grad, second_gain_grad]),
        jnp.concatenate([conv_sums[: CONV + 1], gate_sums[:2], lambda_grad], axis=0),
        gate_blocks_grad,
    )
    gains_grad, chan_grad, gates_grad = lax.psum(
        (small_terms[0], small_terms[1], small_terms[2]), ("seq", "bat")
    )
    slot_grads = jnp.take(
        join_tiles(
            (
                input_weight_grad,
                branch_weight_grad,
                output_weight_grad,
                gate_weight_grad,
                upward_weight_grad,
                down_weight_grad,
            )
        ),
        tile_of_slot,
        axis=0,
        mode="clip",
    )
    own_grads = lax.psum_scatter(slot_grads, ("seq", "bat"), scatter_dimension=0, tiled=True)
    soap_out = soap_update(
        own_grads,
        tile_first,
        tile_second,
        tile_weights,
        basis_left,
        basis_right,
        stat_left,
        stat_right,
    )
    gains_out = adam_update(gains_grad, gains_first, gains_second, norm_gains, small_rate)
    chan_out = adam_update(chan_grad, chan_first, chan_second, chan_params, small_rate)
    gate_out = adam_update(gates_grad, gate_first, gate_second, gate_blocks, learn_rate)
    return (
        block_output[None],
        input_grad[None],
        gains_out[0],
        gains_out[1],
        gains_out[2],
        chan_out[0],
        chan_out[1],
        chan_out[2],
        gate_out[0],
        gate_out[1],
        gate_out[2],
        soap_out[0],
        soap_out[1],
        soap_out[2],
        soap_out[3],
        soap_out[4],
        soap_out[5],
        soap_out[6],
    )


def solution(mesh):
    return jax.shard_map(
        on_device,
        mesh=mesh,
        in_specs=(
            P("bat", "seq", None),
            P("bat", "seq", None),
            P("bat"),
            P(),
            P(),
            P(),
            P(),
            P(),
            P(),
            P(),
            P(),
            P(),
            P(("seq", "bat"), None, None),
            P(("seq", "bat"), None, None),
            P(("seq", "bat"), None, None),
            P(("seq", "bat"), None, None),
            P(("seq", "bat"), None, None),
            P(("seq", "bat"), None, None),
            P(("seq", "bat"), None, None),
            P(),
        ),
        out_specs=(
            P("bat", "seq", None),
            P("bat", "seq", None),
            P(),
            P(),
            P(),
            P(),
            P(),
            P(),
            P(),
            P(),
            P(),
            P(("seq", "bat"), None, None),
            P(("seq", "bat"), None, None),
            P(("seq", "bat"), None, None),
            P(("seq", "bat"), None, None),
            P(("seq", "bat"), None, None),
            P(("seq", "bat"), None, None),
            P(("seq", "bat"), None, None),
        ),
        check_vma=False,
    )
```
